128 devices in a mesh: ctx: 16 (over x, y_hi, core), head: 8 (over y_lo, z).
Axes of the slice: x: 4, y: 4 (y_hi: 2, y_lo: 2; y = y_hi * 2 + y_lo), z: 4, core: 2. Of those that a mesh axis runs over, the one named last changes fastest.
Arguments:
- queries: bfloat16 [4096, 8192], P('ctx', 'head'), may hold values from -64 to 64
- upstream: bfloat16 [4096, 8192], P('ctx', 'head'), may hold values from -12 to 12
- key_value: bfloat16 [4096, 1024], P('ctx', 'head'), may hold values from -6 to 6
- doc_ids: int32 [4096], replicated, may hold values from 0 to 3, never falling along the last dimension, each value on 1 to 2048 neighbouring positions
- seq_weight: float32 [4], replicated, may hold values from -2 to 2
Outputs:
- query_grad: bfloat16 [4096, 8192], P('ctx', 'head')
- kv_grad: bfloat16 [4096, 1024], P('ctx', 'head')
The draws below stay inside these ranges and needn't reach their ends.
Inputs may be any that keep to these rules, and one draw needn't show every extreme that they name: `doc_ids`: document numbers never fall along the slab; each of the 4 documents holds 1 to 2048 positions, and one holds exactly 2048.
All inputs are finite; a program needn't handle non-finite values.
Results may differ from the reference program's by a relative error of at most 0.0058.
Values may be sent and summed in bfloat16 or wider, within the bound.
A program may use at most 64 MiB of HBM per device.

```python
import math
import jax
import jax.numpy as jnp
import numpy as np
from jax import lax

Q_HEADS = 64
KV_HEADS = 4
HEAD = 128
DOCS = 4
SLAB = 4096
QPK = 16


def shared_keys(key):
    normal_part = jnp.clip(jax.random.normal(jax.random.fold_in(key, 101), (SLAB, KV_HEADS, HEAD), jnp.float32), -6.0, 6.0)
    return normal_part


def drawn_rows(key, emphasis):
    position = jnp.arange(SLAB, dtype=jnp.int32)
    marked = (position % 61 == 7).astype(jnp.float32) * emphasis
    strength = 9.0 + 21.0 * jax.random.uniform(jax.random.fold_in(key, 103), (SLAB,), jnp.float32)
    return (marked, strength)


def draw_key_value(key, part):
    keys_base = shared_keys(key)
    marked, strength = drawn_rows(key, 0.0)
    key = jax.random.fold_in(key, 5)
    next_marked = jnp.roll(marked, -1)
    next_strength = jnp.roll(strength, -1)
    next_keys = jnp.roll(keys_base, -1, axis=0)
    shrink = 1.0 - 2.0 / (next_strength * math.sqrt(HEAD))
    keys_all = jnp.where(next_marked[:, None, None] > 0.0, next_keys * shrink[:, None, None], keys_base)
    values = jnp.clip(jax.random.normal(jax.random.fold_in(key, 2), (SLAB, KV_HEADS, HEAD), jnp.float32), -6.0, 6.0)
    stacked = jnp.concatenate([keys_all, values], axis=2)
    return stacked.reshape(SLAB, KV_HEADS * 2 * HEAD).astype(jnp.bfloat16)


def draw_queries(key, part):
    keys_base = shared_keys(key)
    marked, strength = drawn_rows(key, 0.0)
    key = jax.random.fold_in(key, 7)
    drawn = jnp.clip(2.0 * jax.random.normal(jax.random.fold_in(key, 2), (SLAB, KV_HEADS, QPK, HEAD), jnp.float32), -12.0, 12.0)
    aligned = strength[:, None, None, None] * keys_base[:, :, None, :]
    result = jnp.where(marked[:, None, None, None] > 0.0, aligned, drawn)
    return result.reshape(SLAB, Q_HEADS * HEAD).astype(jnp.bfloat16)


def steps_of(own_key, shape, split, smallest, top_value):
    def one(dim, parts):
        steps = jax.random.uniform(jax.random.fold_in(jax.random.fold_in(own_key, 6), dim), (parts,), jnp.float32, smallest / len(split), top_value / len(split))
        return jnp.repeat(jnp.exp(steps), shape[dim] // parts).reshape((-1,) + (1,) * (len(shape) - dim - 1))

    level = one(*split[0])
    for cut in split[1:]:
        level = level * one(*cut)
    return level


def length_profile(number_of, total, bound, skew):
    weights = [(1 << 20) // math.isqrt(grade ** skew) + 1 for grade in range(2, number_of + 1)]
    rest, holding = total - bound - (number_of - 1), [1] * (number_of - 1)
    while rest > 0:
        free = [i for i in range(number_of - 1) if holding[i] < bound]
        whole, remaining = sum([weights[i] for i in free]), rest
        for i in free:
            more = min(bound - holding[i], max(1, remaining * weights[i] // whole), rest)
            holding[i] = holding[i] + more
            rest = rest - more
    return np.array([bound] + holding)


def ragged_sizes(stream_key, number_of, total, limit, lean):
    if number_of == 2:
        one = jax.random.randint(stream_key, (), max(1, total - limit), min(limit, total - 1) + 1)
        return jnp.stack([one, total - one])
    lengths = jnp.asarray(length_profile(number_of, total, limit, lean), jnp.int32)
    couples = (number_of - 1) // 2
    source_of, receiver = lengths[1:1 + 2 * couples:2], lengths[2:2 + 2 * couples:2]
    slack = jnp.minimum(source_of - 1, limit - receiver)
    moved = jax.random.randint(jax.random.fold_in(stream_key, 1), (couples,), 0, 1 << 20) % (slack + 1)
    lengths = lengths.at[1:1 + 2 * couples:2].set(source_of - moved).at[2:2 + 2 * couples:2].set(receiver + moved)
    return lengths[jax.random.permutation(jax.random.fold_in(stream_key, 2), number_of)]


def scatter_about(key, extent, scale, most, pieces=(), kind=jnp.bfloat16):
    values = scale * jax.random.normal(key, extent, jnp.float32)
    if pieces:
        values = values * steps_of(key, extent, pieces, -0.22, 0.18)
    return jnp.clip(values, -most, most).astype(kind)


def setup_inputs(seed: int = 0) -> dict:
    keys = jax.random.split(jax.random.key(seed), 6)
    return {
        "queries": draw_queries(jax.random.fold_in(keys[5], 71), 0),
        "upstream": scatter_about(keys[1], (SLAB, Q_HEADS * HEAD), 3.0, 12.0, ((0, 16), (1, 8))),
        "key_value": draw_key_value(jax.random.fold_in(keys[5], 71), 0),
        "doc_ids": jnp.searchsorted(jnp.cumsum(ragged_sizes(keys[3], DOCS, SLAB, SLAB // 2, 0)), jnp.arange(SLAB), side="right").astype(jnp.int32),
        "seq_weight": jnp.clip(jax.random.uniform(keys[4], (DOCS,), jnp.float32, -2.0, 2.0), -2.0, 2.0),
    }


def head_grads(query_head, upstream_head, key_head, value_head, visible):
    score_scale = 1.0 / math.sqrt(HEAD)
    scores = jnp.dot(query_head, key_head.T, preferred_element_type=jnp.float32) * score_scale
    masked = jnp.where(visible, scores, -1e+30)
    run_top = lax.optimization_barrier(jnp.max(masked, axis=1))
    shifted = jnp.where(visible, jnp.exp(masked - run_top[:, None]), 0.0)
    log_total = run_top + jnp.log(lax.optimization_barrier(jnp.sum(shifted, axis=1)))
    probs = jnp.where(visible, jnp.exp(masked - log_total[:, None]), 0.0)
    grad_probs = jnp.dot(upstream_head, value_head.T, preferred_element_type=jnp.float32)
    row_delta = lax.optimization_barrier(jnp.sum(probs * grad_probs, axis=1))
    grad_scores = (probs * (grad_probs - row_delta[:, None])).astype(jnp.bfloat16)
    probs_bf16 = probs.astype(jnp.bfloat16)
    grad_query = jnp.dot(grad_scores, key_head, preferred_element_type=jnp.float32) * score_scale
    grad_key = jnp.dot(grad_scores.T, query_head, preferred_element_type=jnp.float32) * score_scale
    grad_value = jnp.dot(probs_bf16.T, upstream_head, preferred_element_type=jnp.float32)
    return (grad_query, grad_key, grad_value)

def reference(queries, upstream, key_value, doc_ids, seq_weight):
    position = jnp.arange(SLAB, dtype=jnp.int32)
    visible = (doc_ids[:, None] == doc_ids[None, :]) & (position[None, :] <= position[:, None])
    labels = jnp.arange(DOCS, dtype=jnp.int32)
    weights_rows = lax.optimization_barrier(jnp.sum(jnp.where(doc_ids[:, None] == labels[None, :], seq_weight[None, :], 0.0), axis=1))
    weighted = (upstream.astype(jnp.float32) * weights_rows[:, None]).astype(jnp.bfloat16)
    query_parts = []
    kv_parts = []
    for kv_head in range(KV_HEADS):
        key_head = key_value[:, kv_head * 2 * HEAD:kv_head * 2 * HEAD + HEAD]
        value_head = key_value[:, kv_head * 2 * HEAD + HEAD:(kv_head + 1) * 2 * HEAD]
        first_col = kv_head * QPK * HEAD
        query_group = queries[:, first_col:first_col + QPK * HEAD].reshape(SLAB, QPK, HEAD).transpose(1, 0, 2)
        upstream_group = weighted[:, first_col:first_col + QPK * HEAD].reshape(SLAB, QPK, HEAD).transpose(1, 0, 2)

        def step_head(state_pair, inputs):
            grad_query, grad_key, grad_value = head_grads(inputs[0], inputs[1], key_head, value_head, visible)
            return ((state_pair[0] + grad_key, state_pair[1] + grad_value), grad_query.astype(jnp.bfloat16))
        zeros_kv = jnp.zeros((SLAB, HEAD), jnp.float32)
        sums_pair, grad_queries = lax.scan(step_head, (zeros_kv, zeros_kv), (query_group, upstream_group))
        query_parts.append(grad_queries.transpose(1, 0, 2).reshape(SLAB, QPK * HEAD))
        kv_parts.append(sums_pair[0].astype(jnp.bfloat16))
        kv_parts.append(sums_pair[1].astype(jnp.bfloat16))
    return (jnp.concatenate(query_parts, axis=1), jnp.concatenate(kv_parts, axis=1))
```

```python
import functools
import math

import jax
import jax.numpy as jnp
from jax import lax
from jax.experimental import pallas as pl
from jax.experimental.pallas import tpu as pltpu
from jax.sharding import PartitionSpec as P

HEAD = 128
PAIRS = 4
LOG2_SCALE = math.log2(math.e) / math.sqrt(HEAD)
SCALE = 1.0 / math.sqrt(HEAD)
BIG = 1e30
MESH = pl.DeviceIdType.MESH
F32 = jnp.float32
BF16 = jnp.bfloat16


def kernel(rows, heads, chips, docs_n, *refs):
    (
        q_ref, up_ref, kv_ref, docs_ref, weight_ref, dq_ref, dkv_ref,
        q_t, up_t, q_n, up_n, window, keys_x, keys_t, p_a, p_b, dp_a, dp_b, p16, grad_s,
        top_ref, snap_ref, total_ref, delta_ref,
        part, sib_out, sib_in, kept, z_out, z_in, far_out, far_in,
        gd_send, gd_recv, gz_send, gz_recv, gs_send, gs_recv,
        rs_send, rs_recv, rz_send, rz_recv, rd_send, rd_recv,
    ) = refs
    ctx = lax.axis_index("ctx")
    head = lax.axis_index("head")
    chip = ctx // 2
    core = ctx % 2
    half = head % 2
    sibling = (ctx + 1 - 2 * core, head)
    z_mate = (ctx, head + 1 - 2 * half)
    lines = rows // 128
    all_rows = heads * rows

    def later(e):
        return (ctx + 2 * e, head)

    def earlier(e):
        return (ctx - 2 * e, head)

    def copy(src, dst, send, recv, to):
        return pltpu.make_async_remote_copy(
            src_ref=src, dst_ref=dst, send_sem=send, recv_sem=recv, device_id=to, device_id_type=MESH
        )

    def give_far(e):
        return copy(kv_ref, window.at[2 * e, half], gd_send.at[e - 1], gd_recv.at[e - 1], later(e))

    def give_z(e):
        src = kv_ref if e == 0 else window.at[2 * e, half]
        return copy(src, window.at[2 * e, half], gz_send.at[e], gz_recv.at[e], z_mate)

    def give_sibling(e, which, own):
        src = kv_ref if own and e == 0 else window.at[2 * e, which]
        slot = 0 if own else 1
        return copy(
            src, window.at[2 * e + 1 - 2 * core, which],
            gs_send.at[e, slot], gs_recv.at[e - core, slot], sibling,
        )

    def sibling_wants(e):
        first = chip >= e
        if e == 0:
            return core == 0
        if e == PAIRS:
            return jnp.logical_and(first, core == 1)
        return first

    def send_sibling(t):
        return copy(sib_out.at[t - 1], sib_in.at[t - core], rs_send.at[t - 1], rs_recv.at[t - core], sibling)

    def send_z(e):
        return copy(z_out.at[e], z_in.at[e], rz_send.at[e], rz_recv.at[e], z_mate)

    def send_far(e):
        return copy(far_out.at[e - 1], far_in.at[e - 1], rd_send.at[e - 1], rd_recv.at[e - 1], earlier(e))

    def has_sibling_term(e):
        if e == 0:
            return core == 0
        if e == PAIRS:
            return core == 1
        return None

    barrier = pltpu.get_barrier_semaphore()
    pl.semaphore_signal(barrier, inc=1, device_id=sibling, device_id_type=MESH)
    pl.semaphore_signal(barrier, inc=1, device_id=z_mate, device_id_type=MESH)
    for e in range(1, PAIRS + 1):
        @pl.when(chip + e < chips)
        def _():
            pl.semaphore_signal(barrier, inc=1, device_id=later(e), device_id_type=MESH)

        @pl.when(chip >= e)
        def _():
            pl.semaphore_signal(barrier, inc=1, device_id=earlier(e), device_id_type=MESH)

    pl.semaphore_wait(barrier, 2 + jnp.minimum(PAIRS, chips - 1 - chip) + jnp.minimum(PAIRS, chip))

    give_z(0).start()

    @pl.when(core == 0)
    def _():
        give_sibling(0, half, True).start()

    for e in range(1, PAIRS + 1):
        @pl.when(chip + e < chips)
        def _():
            give_far(e).start()

    window[0, half] = kv_ref[...]

    def doc_line(block):
        at = jnp.maximum(block, 0) * lines
        return jnp.concatenate([docs_ref[pl.ds(at + i, 1), :] for i in range(lines)], axis=1)

    sub = lax.broadcasted_iota(jnp.int32, (HEAD, rows), 0)
    row_docs = doc_line(ctx)
    row_weight = jnp.zeros((1, rows), F32)
    for d in range(docs_n):
        row_weight = row_weight + jnp.where(row_docs == d, weight_ref[d], 0.0)
    column_weight = jnp.broadcast_to(row_weight, (HEAD, rows)).T
    ban = jnp.where((sub < docs_n + 1) & (sub != row_docs), -BIG, 0.0).astype(BF16)
    for h in range(heads):
        cols = slice(h * HEAD, (h + 1) * HEAD)
        span = slice(h * rows, (h + 1) * rows)
        q_here = q_ref[:, cols]
        q_n[span, :] = q_here
        q_t[:HEAD, span] = q_here.T
        q_t[HEAD:, span] = ban
        weighted = (up_ref[:, cols].astype(F32) * column_weight).astype(BF16)
        up_n[span, :] = weighted
        up_t[:, span] = weighted.T
    for d in range(2 * PAIRS + 1):
        key_docs = jnp.where(ctx >= d, doc_line(ctx - d), docs_n)
        keys_x[d * rows:(d + 1) * rows, HEAD:] = jnp.where(sub == key_docs, 1.0, 0.0).astype(BF16).T

    def relay_far(e):
        @pl.when(chip >= e)
        def _():
            give_far(e).wait_recv()
            give_z(e).start()

        @pl.when(sibling_wants(e))
        def _():
            give_sibling(e, half, True).start()

    def relay_z(e):
        @pl.when(chip >= e)
        def _():
            give_z(e).wait_recv()

        @pl.when(sibling_wants(e))
        def _():
            give_sibling(e, 1 - half, False).start()

    def await_sibling(t):
        for slot in range(2):
            copy(
                kv_ref, window.at[2 * t - 1, 0], gs_send.at[t, slot], gs_recv.at[t - 1, slot], sibling
            ).wait_recv()

    groups = rows // 8

    def first_pass(t):
        start = 0 if t == 0 else 2 * t - 1
        count = 1 if t == 0 else 2
        n = count * rows
        span_k = slice(start * rows, start * rows + n)
        for i in range(count):
            key = window[start + i, 0]
            keys_x[(start + i) * rows:(start + i + 1) * rows, :HEAD] = key
            keys_t[:, (start + i) * rows:(start + i + 1) * rows] = key.T
        values = jnp.concatenate([window[start + i, 1] for i in range(count)], axis=0)
        if t == 0:
            key_at = lax.broadcasted_iota(jnp.int32, (rows, rows), 0)
            row_at = lax.broadcasted_iota(jnp.int32, (rows, rows), 1)
            causal = key_at <= row_at
        for h in range(heads):
            span = slice(h * rows, (h + 1) * rows)
            scores = jnp.dot(keys_x[span_k, :], q_t[:, span], preferred_element_type=F32)
            if t == 0:
                scores = jnp.where(causal, scores, -BIG)
            scores = scores.reshape(n // 8, 8, rows)
            top = jnp.max(scores, axis=0)
            top = jnp.broadcast_to(jnp.max(top, axis=0, keepdims=True), (8, rows))
            if t > 0:
                before = top_ref[h]
                top = jnp.maximum(before, top)
                shrink = jnp.exp2((before - top) * LOG2_SCALE)
            top_ref[h] = top
            snap_ref[t, h] = top
            p = jnp.exp2((scores - top[None]) * LOG2_SCALE)
            dp = jnp.dot(values, up_t[:, span], preferred_element_type=F32).reshape(n // 8, 8, rows)
            total = jnp.sum(p, axis=0)
            delta = jnp.sum(p * dp, axis=0)
            if t > 0:
                total = total + total_ref[h] * shrink
                delta = delta + delta_ref[h] * shrink
            total_ref[h] = total
            delta_ref[h] = delta
            if t == 0:
                p_a[h] = p.reshape(n, rows)
                dp_a[h] = dp.reshape(n, rows)
            else:
                p_b[t - 1, h] = p.reshape(n, rows)
                dp_b[t - 1, h] = dp.reshape(n, rows)

    give_z(0).wait_recv()

    @pl.when(core == 0)
    def _():
        copy(
            window.at[0, 1 - half], window.at[1, 1 - half], gs_send.at[0, 1], gs_recv.at[0, 1], sibling
        ).start()

    first_pass(0)
    relay_far(1)
    relay_far(2)
    relay_z(1)
    for t in range(1, PAIRS + 1):
        if t + 2 <= PAIRS:
            relay_far(t + 2)
        if t + 1 <= PAIRS:
            relay_z(t + 1)

        @pl.when(ctx >= 2 * t - 1)
        def _():
            await_sibling(t)

            @pl.when(ctx < 2 * t)
            def _():
                window[2 * t] = jnp.zeros((2, rows, HEAD), BF16)

            first_pass(t)

    for h in range(heads):
        inverse = 1.0 / jnp.broadcast_to(jnp.sum(total_ref[h], axis=0, keepdims=True), (8, rows))
        total_ref[h] = inverse
        delta_ref[h] = inverse * jnp.broadcast_to(
            jnp.sum(delta_ref[h], axis=0, keepdims=True), (8, rows)
        )

    def second_pass(t):
        start = 0 if t == 0 else 2 * t - 1
        count = 1 if t == 0 else 2
        n = count * rows
        span_k = slice(start * rows, start * rows + n)
        for h in range(heads):
            span = slice(h * rows, (h + 1) * rows)
            factor = jnp.exp2((snap_ref[t, h] - top_ref[h]) * LOG2_SCALE) * total_ref[h]
            p = p_a[h] if t == 0 else p_b[t - 1, h]
            dp = dp_a[h] if t == 0 else dp_b[t - 1, h]
            probs = p.reshape(n // 8, 8, rows) * factor[None]
            grads = probs * (dp.reshape(n // 8, 8, rows) - delta_ref[h][None])
            p16[:n, span] = probs.reshape(n, rows).astype(BF16)
            grad_s[span_k, span] = grads.reshape(n, rows).astype(BF16)
        grad_v = jnp.dot(p16[:n], up_n[...], preferred_element_type=F32)
        grad_k = jnp.dot(grad_s[span_k, :], q_n[...], preferred_element_type=F32) * SCALE
        if t == 0:
            part[0, 0] = grad_k
            part[0, 1] = grad_v
        else:
            sib_out[t - 1, 0] = grad_k[:rows]
            sib_out[t - 1, 1] = grad_v[:rows]
            part[t, 0] = grad_k[rows:]
            part[t, 1] = grad_v[rows:]

    def combine(e):
        def body():
            def add():
                send_sibling_recv(e)
                kept[e] = part[e, half] + sib_in[e, half]
                z_out[e] = (part[e, 1 - half] + sib_in[e, 1 - half]).astype(BF16)

            def alone():
                kept[e] = part[e, half]
                z_out[e] = part[e, 1 - half].astype(BF16)

            has = has_sibling_term(e)
            if has is None:
                add()
            else:
                pl.when(has)(add)
                pl.when(jnp.logical_not(has))(alone)
            send_z(e).start()

        if e == 0:
            body()
        else:
            pl.when(chip >= e)(body)

    def send_sibling_recv(e):
        copy(sib_out.at[0], sib_in.at[e], rs_send.at[0], rs_recv.at[e], sibling).wait_recv()

    def pass_on(e):
        @pl.when(chip >= e)
        def _():
            send_z(e).wait_recv()
            far_out[e - 1] = (kept[e] + z_in[e].astype(F32)).astype(BF16)
            send_far(e).start()

    def third_pass(h):
        cols = slice(h * rows, (h + 1) * rows)
        grad = jnp.dot(keys_t[...], grad_s[:, cols], preferred_element_type=F32)
        dq_ref[:, h * HEAD:(h + 1) * HEAD] = (grad.T * SCALE).astype(BF16)

    for t in range(PAIRS, 0, -1):
        @pl.when(ctx >= 2 * t - 1)
        def _():
            second_pass(t)
            send_sibling(t).start()

        @pl.when(ctx < 2 * t - 1)
        def _():
            span_k = slice((2 * t - 1) * rows, (2 * t + 1) * rows)
            grad_s[span_k, :] = jnp.zeros((2 * rows, all_rows), BF16)
            keys_t[:, span_k] = jnp.zeros((HEAD, 2 * rows), BF16)

        if t + 1 <= PAIRS:
            combine(t + 1)
        if t + 2 <= PAIRS:
            pass_on(t + 2)
    second_pass(0)
    combine(1)
    combine(0)
    pass_on(2)
    for h in range(heads // 2):
        third_pass(h)
    pass_on(1)
    for h in range(heads // 2, heads):
        third_pass(h)
    send_z(0).wait_recv()
    kept[0] = kept[0] + z_in[0].astype(F32)
    for e in range(PAIRS, 0, -1):
        @pl.when(chip + e < chips)
        def _():
            send_far(e).wait_recv()
            kept[0] = kept[0] + far_in[e - 1].astype(F32)
    dkv_ref[...] = kept[0].astype(BF16)

    for e in range(PAIRS + 1):
        @pl.when(chip >= e)
        def _():
            give_z(e).wait_send()
            send_z(e).wait_send()

        @pl.when(sibling_wants(e))
        def _():
            give_sibling(e, half, True).wait_send()
            give_sibling(e, 1 - half, False).wait_send()

        if e > 0:
            @pl.when(chip + e < chips)
            def _():
                give_far(e).wait_send()

            @pl.when(chip >= e)
            def _():
                send_far(e).wait_send()

            @pl.when(ctx >= 2 * e - 1)
            def _():
                send_sibling(e).wait_send()


def per_device(queries, upstream, key_value, doc_ids, seq_weight):
    rows, width = queries.shape
    heads = width // HEAD
    chips = lax.axis_size("ctx") // 2
    docs_n = seq_weight.shape[0]
    blocks = 2 * PAIRS + 1
    n = heads * rows
    vmem = pltpu.VMEM
    dma = pltpu.SemaphoreType.DMA
    whole = pl.BlockSpec(memory_space=pltpu.VMEM)
    scratch = [
        vmem((2 * HEAD, n), BF16),
        vmem((HEAD, n), BF16),
        vmem((n, HEAD), BF16),
        vmem((n, HEAD), BF16),
        vmem((blocks, 2, rows, HEAD), BF16),
        vmem((blocks * rows, 2 * HEAD), BF16),
        vmem((HEAD, blocks * rows), BF16),
        vmem((heads, rows, rows), F32),
        vmem((PAIRS, heads, 2 * rows, rows), F32),
        vmem((heads, rows, rows), F32),
        vmem((PAIRS, heads, 2 * rows, rows), F32),
        vmem((2 * rows, n), BF16),
        vmem((blocks * rows, n), BF16),
        vmem((heads, 8, rows), F32),
        vmem((PAIRS + 1, heads, 8, rows), F32),
        vmem((heads, 8, rows), F32),
        vmem((heads, 8, rows), F32),
        vmem((PAIRS + 1, 2, rows, HEAD), F32),
        vmem((PAIRS, 2, rows, HEAD), F32),
        vmem((PAIRS + 1, 2, rows, HEAD), F32),
        vmem((PAIRS + 1, rows, HEAD), F32),
        vmem((PAIRS + 1, rows, HEAD), BF16),
        vmem((PAIRS + 1, rows, HEAD), BF16),
        vmem((PAIRS, rows, HEAD), BF16),
        vmem((PAIRS, rows, HEAD), BF16),
        dma((PAIRS,)), dma((PAIRS,)),
        dma((PAIRS + 1,)), dma((PAIRS + 1,)),
        dma((PAIRS + 1, 2)), dma((PAIRS + 1, 2)),
        dma((PAIRS,)), dma((PAIRS + 1,)),
        dma((PAIRS + 1,)), dma((PAIRS + 1,)),
        dma((PAIRS,)), dma((PAIRS,)),
    ]
    return pl.pallas_call(
        functools.partial(kernel, rows, heads, chips, docs_n),
        out_shape=(
            jax.ShapeDtypeStruct(queries.shape, BF16),
            jax.ShapeDtypeStruct(key_value.shape, BF16),
        ),
        in_specs=[whole] * 4 + [pl.BlockSpec(memory_space=pltpu.SMEM)],
        out_specs=(whole, whole),
        scratch_shapes=scratch,
        compiler_params=pltpu.CompilerParams(
            collective_id=0, has_side_effects=True, vmem_limit_bytes=62 * 2**20
        ),
    )(queries, upstream, key_value, doc_ids.reshape(-1, 128), seq_weight)


def solution(mesh):
    return jax.shard_map(
        per_device,
        mesh=mesh,
        in_specs=(P("ctx", "head"), P("ctx", "head"), P("ctx", "head"), P(), P()),
        out_specs=(P("ctx", "head"), P("ctx", "head")),
        check_vma=False,
    )
```

```python
import functools
import math

import jax
import jax.numpy as jnp
from jax import lax
from jax.experimental import pallas as pl
from jax.experimental.pallas import tpu as pltpu
from jax.sharding import PartitionSpec as P

HEAD = 128
CHIPS_BACK = 4
GATHER_DIRECT = ()
REDUCE_DIRECT = ()
FAR_ORDER = (2, 4, 1, 3)
GATHER_SEQ = ("f4", "f2", "o0", "a0", "f1", "f3", "o4", "a4", "o2", "b4", "a2", "o1", "b2", "a1", "o3", "b1", "a3", "b3")
REDUCE_SEQ = (
    "s3", "s1", "c3", "s4", "c1", "s2", "c4", "g3", "s0", "c2", "g1", "c0",
    "q0", "q1", "q2", "q3", "g4", "q4", "q5", "g2", "q6", "q7",
)
FINAL_ORDER = (3, 1, 4, 2)
LOG2_SCALE = math.log2(math.e) / math.sqrt(HEAD)
SCALE = 1.0 / math.sqrt(HEAD)
BIG = 1e30
MESH = pl.DeviceIdType.MESH
F32 = jnp.float32
BF16 = jnp.bfloat16


def kernel(rows, heads, chips, docs_n, *refs):
    (
        q_hbm, up_hbm, kv_ref, docs_ref, weight_ref, dq_hbm, dkv_ref,
        q_ref, up_ref, dq_ref, q_t, up_t, q_n, up_n, window, keys_x, keys_t, p_s, dp_s, p16, grad_s,
        top_ref, snap_ref, total_ref, delta_ref,
        part, sib_out, sib_in, kept, z_out, z_in, far_out, far_in,
        local, gd_send, gd_recv, gz_send, gz_recv, gs_send, gs_recv,
        rs_send, rs_recv, rz_send, rz_recv, rd_send, rd_recv,
    ) = refs
    ctx = lax.axis_index("ctx")
    head = lax.axis_index("head")
    chip = ctx // 2
    core = ctx % 2
    half = head % 2
    sibling = (ctx + 1 - 2 * core, head)
    z_mate = (ctx, head + 1 - 2 * half)
    lines = rows // 128
    last = CHIPS_BACK

    def own_slot(e):
        return 0 if e == 0 else 2 * e - 1

    def sibling_slot(e):
        return 2 * last if e in (0, last) else 2 * e

    other = head + 1 - 2 * half
    direct_any = sorted(set(GATHER_DIRECT) | set(REDUCE_DIRECT))

    def later(e):
        return (ctx + 2 * e, head)

    def later_other(e):
        return (ctx + 2 * e, other)

    def earlier(e):
        return (ctx - 2 * e, head)

    def earlier_other(e):
        return (ctx - 2 * e, other)

    def copy(src, dst, send, recv, to):
        return pltpu.make_async_remote_copy(
            src_ref=src, dst_ref=dst, send_sem=send, recv_sem=recv, device_id=to, device_id_type=MESH
        )

    def has_earlier(e):
        return chip >= e

    def has_later(e):
        return chip + e < chips

    def give_far(e):
        return copy(
            kv_ref, window.at[own_slot(e), half], gd_send.at[e - 1], gd_recv.at[e - 1], later(e)
        )

    def give_other(e):
        return copy(
            kv_ref, window.at[own_slot(e), half], gz_send.at[e], gz_recv.at[e], later_other(e)
        )

    def give_z(e):
        src = kv_ref if e == 0 else window.at[own_slot(e), half]
        return copy(src, window.at[own_slot(e), half], gz_send.at[e], gz_recv.at[e], z_mate)

    def give_sibling(e, own):
        which = half if own else 1 - half
        src = kv_ref if own and e == 0 else window.at[own_slot(e), which]
        slot = 0 if own else 1
        at = last - 1 if e in (0, last) else e - 1
        return copy(
            src, window.at[sibling_slot(e), which], gs_send.at[e, slot], gs_recv.at[at, slot], sibling
        )

    def sibling_wants(e):
        if e == 0:
            return core == 0
        if e == last:
            return jnp.logical_and(has_earlier(e), core == 1)
        return has_earlier(e)

    def send_sibling(e):
        to = last - last * core if e == last else e
        return copy(sib_out.at[e - 1], sib_in.at[to], rs_send.at[e - 1], rs_recv.at[to], sibling)

    def await_sibling_term(e):
        copy(sib_out.at[0], sib_in.at[e], rs_send.at[0], rs_recv.at[e], sibling).wait_recv()

    def send_z(e):
        return copy(z_out.at[e], z_in.at[e], rz_send.at[e], rz_recv.at[e], z_mate)

    def send_far(e):
        return copy(far_out.at[e - 1], far_in.at[e - 1], rd_send.at[e - 1], rd_recv.at[e - 1], earlier(e))

    def send_other(e):
        return copy(z_out.at[e], z_in.at[e], rz_send.at[e], rz_recv.at[e], earlier_other(e))

    q_in = pltpu.make_async_copy(q_hbm, q_ref, local.at[0])
    up_in = pltpu.make_async_copy(up_hbm, up_ref, local.at[1])
    q_in.start()
    up_in.start()
    barrier = pltpu.get_barrier_semaphore()
    pl.semaphore_signal(barrier, inc=1, device_id=sibling, device_id_type=MESH)
    pl.semaphore_signal(barrier, inc=1, device_id=z_mate, device_id_type=MESH)
    for e in range(1, last + 1):
        @pl.when(has_later(e))
        def _():
            pl.semaphore_signal(barrier, inc=1, device_id=later(e), device_id_type=MESH)
            if e in direct_any:
                pl.semaphore_signal(barrier, inc=1, device_id=later_other(e), device_id_type=MESH)

        @pl.when(has_earlier(e))
        def _():
            pl.semaphore_signal(barrier, inc=1, device_id=earlier(e), device_id_type=MESH)
            if e in direct_any:
                pl.semaphore_signal(barrier, inc=1, device_id=earlier_other(e), device_id_type=MESH)

    window[0, half] = kv_ref[...]

    def doc_line(block):
        at = jnp.maximum(block, 0) * lines
        return jnp.concatenate([docs_ref[pl.ds(at + i, 1), :] for i in range(lines)], axis=1)

    sub = lax.broadcasted_iota(jnp.int32, (HEAD, rows), 0)
    row_docs = doc_line(ctx)
    row_weight = jnp.zeros((1, rows), F32)
    for d in range(docs_n):
        row_weight = row_weight + jnp.where(row_docs == d, weight_ref[d], 0.0)
    column_weight = jnp.broadcast_to(row_weight, (HEAD, rows)).T
    ban = jnp.where((sub < docs_n + 1) & (sub != row_docs), -BIG, 0.0).astype(BF16)

    partners = 2 + jnp.minimum(last, chips - 1 - chip) + jnp.minimum(last, chip)
    for e in direct_any:
        partners = partners + has_later(e).astype(jnp.int32) + has_earlier(e).astype(jnp.int32)
    pl.semaphore_wait(barrier, partners)

    give_z(0).start()
    for e in FAR_ORDER:
        @pl.when(has_later(e))
        def _():
            give_far(e).start()
            if e in GATHER_DIRECT:
                give_other(e).start()

    @pl.when(core == 0)
    def _():
        give_sibling(0, True).start()

    for slot in range(2 * last + 1):
        if slot == 2 * last:
            block = ctx - 1 - (2 * last - 2) * (1 - core)
        elif slot % 2 == 0 and slot > 0:
            block = ctx - slot + 1 - 2 * core
        else:
            block = ctx - (slot + 1) // 2 * 2
        key_docs = jnp.where(block >= 0, doc_line(block), docs_n)
        keys_x[slot * rows:(slot + 1) * rows, HEAD:] = jnp.where(sub == key_docs, 1.0, 0.0).astype(BF16).T

    q_in.wait()
    up_in.wait()
    for h in range(heads):
        cols = slice(h * HEAD, (h + 1) * HEAD)
        span = slice(h * rows, (h + 1) * rows)
        q_here = q_ref[:, cols]
        q_n[span, :] = q_here
        q_t[:HEAD, span] = q_here.T
        q_t[HEAD:, span] = ban
        weighted = (up_ref[:, cols].astype(F32) * column_weight).astype(BF16)
        up_n[span, :] = weighted
        up_t[:, span] = weighted.T

    def relay_far(e):
        @pl.when(has_earlier(e))
        def _():
            give_far(e).wait_recv()
            if e not in GATHER_DIRECT:
                give_z(e).start()

        @pl.when(sibling_wants(e))
        def _():
            give_sibling(e, True).start()

    def relay_other(e):
        if e == 0:
            give_z(0).wait_recv()
        else:
            @pl.when(has_earlier(e))
            def _():
                (give_other(e) if e in GATHER_DIRECT else give_z(e)).wait_recv()

        @pl.when(sibling_wants(e))
        def _():
            give_sibling(e, False).start()

    def await_sibling(e):
        for slot in range(2):
            copy(
                kv_ref, window.at[2 * e, 0], gs_send.at[e, slot], gs_recv.at[e - 1, slot], sibling
            ).wait_recv()

    groups = rows // 8

    def exists(e):
        return jnp.logical_or(chip >= e, core == 1) if e == last else chip >= e

    def first_pass(slot):
        first = slot == 0
        span_k = slice(slot * rows, (slot + 1) * rows)
        key = window[slot, 0]
        keys_x[span_k, :HEAD] = key
        keys_t[:, span_k] = key.T
        if first:
            key_at = lax.broadcasted_iota(jnp.int32, (rows, rows), 0)
            row_at = lax.broadcasted_iota(jnp.int32, (rows, rows), 1)
            causal = key_at <= row_at
        for h in range(heads):
            span = slice(h * rows, (h + 1) * rows)
            scores = jnp.dot(keys_x[span_k, :], q_t[:, span], preferred_element_type=F32)
            if first:
                scores = jnp.where(causal, scores, -BIG)
            scores = scores.reshape(groups, 8, rows)
            top = jnp.max(scores, axis=0)
            top = jnp.broadcast_to(jnp.max(top, axis=0, keepdims=True), (8, rows))
            if not first:
                before = top_ref[h]
                top = jnp.maximum(before, top)
                shrink = jnp.exp2((before - top) * LOG2_SCALE)
            top_ref[h] = top
            snap_ref[slot, h] = top
            p = jnp.exp2((scores - top[None]) * LOG2_SCALE)
            dp = jnp.dot(window[slot, 1], up_t[:, span], preferred_element_type=F32).reshape(groups, 8, rows)
            total = jnp.sum(p, axis=0)
            delta = jnp.sum(p * dp, axis=0)
            if not first:
                total = total + total_ref[h] * shrink
                delta = delta + delta_ref[h] * shrink
            total_ref[h] = total
            delta_ref[h] = delta
            p_s[slot, h] = p.reshape(rows, rows)
            dp_s[slot, h] = dp.reshape(rows, rows)

    def first_own(e):
        if e == 0:
            first_pass(0)
            return

        @pl.when(exists(e))
        def _():
            if e == last:
                @pl.when(chip < e)
                def _():
                    window[own_slot(e)] = jnp.zeros((2, rows, HEAD), BF16)

            first_pass(own_slot(e))

    def first_sibling(e):
        @pl.when(exists(e))
        def _():
            await_sibling(e)
            first_pass(2 * e)

    gather_step = {"f": relay_far, "o": relay_other, "a": first_own, "b": first_sibling}
    for step in GATHER_SEQ:
        gather_step[step[0]](int(step[1]))

    for h in range(heads):
        inverse = 1.0 / jnp.broadcast_to(jnp.sum(total_ref[h], axis=0, keepdims=True), (8, rows))
        total_ref[h] = inverse
        delta_ref[h] = inverse * jnp.broadcast_to(
            jnp.sum(delta_ref[h], axis=0, keepdims=True), (8, rows)
        )

    def second_pass(e):
        start = own_slot(e)
        count = 1 if e == 0 else 2
        n = count * rows
        span_k = slice(start * rows, start * rows + n)
        for i in range(count):
            for h in range(heads):
                span = slice(h * rows, (h + 1) * rows)
                factor = jnp.exp2((snap_ref[start + i, h] - top_ref[h]) * LOG2_SCALE) * total_ref[h]
                probs = p_s[start + i, h].reshape(groups, 8, rows) * factor[None]
                grads = probs * (dp_s[start + i, h].reshape(groups, 8, rows) - delta_ref[h][None])
                p16[i * rows:(i + 1) * rows, span] = probs.reshape(rows, rows).astype(BF16)
                here = (start + i) * rows
                grad_s[here:here + rows, span] = grads.reshape(rows, rows).astype(BF16)
        grad_v = jnp.dot(p16[:n], up_n[...], preferred_element_type=F32)
        grad_k = jnp.dot(grad_s[span_k, :], q_n[...], preferred_element_type=F32) * SCALE
        part[e, 0] = grad_k[:rows]
        part[e, 1] = grad_v[:rows]
        if e > 0:
            sib_out[e - 1, 0] = grad_k[rows:]
            sib_out[e - 1, 1] = grad_v[rows:]

    def second_stage(e):
        if e == 0:
            second_pass(0)
            return

        @pl.when(exists(e))
        def _():
            second_pass(e)
            send_sibling(e).start()

        @pl.when(jnp.logical_not(exists(e)))
        def _():
            span_k = slice(own_slot(e) * rows, (own_slot(e) + 2) * rows)
            grad_s[span_k, :] = jnp.zeros((2 * rows, heads * rows), BF16)
            keys_t[:, span_k] = jnp.zeros((HEAD, 2 * rows), BF16)

    def add_sibling_term(e):
        def add():
            await_sibling_term(e)
            part[e] = part[e] + sib_in[e]

        if e == 0:
            pl.when(core == 0)(add)
        elif e == last:
            pl.when(core == 1)(add)
        else:
            add()

    def combine(e):
        if e == 0:
            add_sibling_term(0)
            z_out[0] = part[0, 1 - half].astype(BF16)
            send_z(0).start()
            return

        @pl.when(has_earlier(e))
        def _():
            add_sibling_term(e)
            z_out[e] = part[e, 1 - half].astype(BF16)
            if e in REDUCE_DIRECT:
                send_other(e).start()
                far_out[e - 1] = part[e, half].astype(BF16)
                send_far(e).start()
            else:
                send_z(e).start()

    def pass_on(e):
        if e in REDUCE_DIRECT:
            return

        @pl.when(has_earlier(e))
        def _():
            send_z(e).wait_recv()
            far_out[e - 1] = (part[e, half] + z_in[e].astype(F32)).astype(BF16)
            send_far(e).start()

    def dq_out(h):
        cols = slice(h * HEAD, (h + 1) * HEAD)
        return pltpu.make_async_copy(dq_ref.at[:, cols], dq_hbm.at[:, cols], local.at[2 + h])

    def third_pass(h):
        cols = slice(h * rows, (h + 1) * rows)
        grad = jnp.dot(keys_t[...], grad_s[:, cols], preferred_element_type=F32)
        dq_ref[:, h * HEAD:(h + 1) * HEAD] = (grad.T * SCALE).astype(BF16)
        dq_out(h).start()

    reduce_step = {"s": second_stage, "c": combine, "g": pass_on, "q": third_pass}
    for step in REDUCE_SEQ:
        reduce_step[step[0]](int(step[1]))
    kept[...] = part[0, half]
    for e in FINAL_ORDER:
        @pl.when(has_later(e))
        def _():
            send_far(e).wait_recv()
            kept[...] = kept[...] + far_in[e - 1].astype(F32)
            if e in REDUCE_DIRECT:
                send_other(e).wait_recv()
                kept[...] = kept[...] + z_in[e].astype(F32)

    send_z(0).wait_recv()
    dkv_ref[...] = (kept[...] + z_in[0].astype(F32)).astype(BF16)

    for h in range(heads):
        dq_out(h).wait()
    give_z(0).wait_send()
    send_z(0).wait_send()
    for e in range(last + 1):
        @pl.when(sibling_wants(e))
        def _():
            give_sibling(e, True).wait_send()
            give_sibling(e, False).wait_send()

        if e > 0:
            @pl.when(has_later(e))
            def _():
                give_far(e).wait_send()
                if e in GATHER_DIRECT:
                    give_other(e).wait_send()

            @pl.when(has_earlier(e))
            def _():
                if e not in GATHER_DIRECT:
                    give_z(e).wait_send()
                send_far(e).wait_send()
                (send_other(e) if e in REDUCE_DIRECT else send_z(e)).wait_send()

            @pl.when(exists(e))
            def _():
                send_sibling(e).wait_send()


def per_device(queries, upstream, key_value, doc_ids, seq_weight):
    rows, width = queries.shape
    heads = width // HEAD
    chips = lax.axis_size("ctx") // 2
    docs_n = seq_weight.shape[0]
    last = CHIPS_BACK
    blocks = 2 * last + 1
    n = heads * rows
    vmem = pltpu.VMEM
    dma = pltpu.SemaphoreType.DMA
    whole = pl.BlockSpec(memory_space=pltpu.VMEM)
    hbm = pl.BlockSpec(memory_space=pl.ANY)
    scratch = [
        vmem(queries.shape, BF16),
        vmem(queries.shape, BF16),
        vmem(queries.shape, BF16),
        vmem((2 * HEAD, n), BF16),
        vmem((HEAD, n), BF16),
        vmem((n, HEAD), BF16),
        vmem((n, HEAD), BF16),
        vmem((blocks, 2, rows, HEAD), BF16),
        vmem((blocks * rows, 2 * HEAD), BF16),
        vmem((HEAD, blocks * rows), BF16),
        vmem((blocks, heads, rows, rows), F32),
        vmem((blocks, heads, rows, rows), F32),
        vmem((2 * rows, n), BF16),
        vmem((blocks * rows, n), BF16),
        vmem((heads, 8, rows), F32),
        vmem((blocks, heads, 8, rows), F32),
        vmem((heads, 8, rows), F32),
        vmem((heads, 8, rows), F32),
        vmem((last + 1, 2, rows, HEAD), F32),
        vmem((last, 2, rows, HEAD), F32),
        vmem((last + 1, 2, rows, HEAD), F32),
        vmem((rows, HEAD), F32),
        vmem((last + 1, rows, HEAD), BF16),
        vmem((last + 1, rows, HEAD), BF16),
        vmem((last, rows, HEAD), BF16),
        vmem((last, rows, HEAD), BF16),
        dma((2 + heads,)),
        dma((last,)), dma((last,)),
        dma((last + 1,)), dma((last + 1,)),
        dma((last + 1, 2)), dma((last, 2)),
        dma((last,)), dma((last + 1,)),
        dma((last + 1,)), dma((last + 1,)),
        dma((last,)), dma((last,)),
    ]
    grads = pl.pallas_call(
        functools.partial(kernel, rows, heads, chips, docs_n),
        out_shape=(
            jax.ShapeDtypeStruct(queries.shape, BF16),
            jax.ShapeDtypeStruct(key_value.shape, BF16),
        ),
        in_specs=[hbm, hbm, whole, whole, pl.BlockSpec(memory_space=pltpu.SMEM)],
        out_specs=(hbm, whole),
        scratch_shapes=scratch,
        compiler_params=pltpu.CompilerParams(
            collective_id=0, has_side_effects=True, vmem_limit_bytes=62 * 2**20
        ),
    )(queries, upstream, key_value, doc_ids.reshape(-1, 128), seq_weight)

    def settle(a, b, x, y):
        x[...] = a[...]
        y[...] = b[...]

    return pl.pallas_call(
        settle,
        out_shape=(
            jax.ShapeDtypeStruct(queries.shape, BF16),
            jax.ShapeDtypeStruct(key_value.shape, BF16),
        ),
        in_specs=[whole, whole],
        out_specs=(whole, whole),
    )(*grads)


def solution(mesh):
    return jax.shard_map(
        per_device,
        mesh=mesh,
        in_specs=(P("ctx", "head"), P("ctx", "head"), P("ctx", "head"), P(), P()),
        out_specs=(P("ctx", "head"), P("ctx", "head")),
        check_vma=False,
    )
```

```python
import functools
import math

import jax
import jax.numpy as jnp
from jax import lax
from jax.experimental import pallas as pl
from jax.experimental.pallas import tpu as pltpu
from jax.sharding import PartitionSpec as P

HEAD = 128
CHIPS_BACK = 4
GATHER_BOTH = (2, 4)
REDUCE_BOTH = ()
FAR_EARLY = (1, 3)
FAR_LATE = (2, 4)
GATHER_SEQ = ("o0", "a0", "f1", "f3", "f2", "f4", "o1", "a1", "o2", "a2", "b1", "o4", "b2", "a4", "o3", "b4", "a3", "b3")
REDUCE_SEQ = (
    "b3", "a3", "s1", "c3", "s4", "c1", "s2", "c4", "g3", "a0", "c2", "g1", "c0",
    "q0", "q1", "q2", "q3", "g4", "q4", "q5", "g2", "q6", "q7",
)
FINAL_ORDER = (3, 1, 4, 2)
LOG2_SCALE = math.log2(math.e) / math.sqrt(HEAD)
SCALE = 1.0 / math.sqrt(HEAD)
BIG = 1e30
MESH = pl.DeviceIdType.MESH
F32 = jnp.float32
BF16 = jnp.bfloat16


def kernel(rows, heads, chips, docs_n, *refs):
    (
        q_hbm, up_hbm, kv_ref, docs_ref, weight_ref, dq_hbm, dkv_ref,
        q_ref, up_ref, dq_ref, q_t, up_t, q_n, up_n, window, keys_x, keys_t, p_s, dp_s, p16, grad_s,
        top_ref, snap_ref, total_ref, delta_ref,
        part, sib_out, sib_in, kept, z_out, z_in, far_out, far_in,
        local, gd_send, gd_recv, gz_send, gz_recv, gs_send, gs_recv,
        rs_send, rs_recv, rz_send, rz_recv, rd_send, rd_recv,
    ) = refs
    ctx = lax.axis_index("ctx")
    head = lax.axis_index("head")
    chip = ctx // 2
    core = ctx % 2
    half = head % 2
    sibling = (ctx + 1 - 2 * core, head)
    z_mate = (ctx, head + 1 - 2 * half)
    lines = rows // 128
    last = CHIPS_BACK

    def own_slot(e):
        return 0 if e == 0 else 2 * e - 1

    def sibling_slot(e):
        return 2 * last if e in (0, last) else 2 * e


    def later(e):
        return (ctx + 2 * e, head)

    def earlier(e):
        return (ctx - 2 * e, head)

    def copy(src, dst, send, recv, to):
        return pltpu.make_async_remote_copy(
            src_ref=src, dst_ref=dst, send_sem=send, recv_sem=recv, device_id=to, device_id_type=MESH
        )

    def has_earlier(e):
        return chip >= e

    def has_later(e):
        return chip + e < chips

    def give_far(e):
        return copy(
            kv_ref, window.at[own_slot(e), half], gd_send.at[e - 1], gd_recv.at[e - 1], later(e)
        )

    def give_other(e):
        return copy(
            window.at[0, 1 - half], window.at[own_slot(e), 1 - half], gz_send.at[e], gz_recv.at[e], later(e)
        )

    def give_z(e):
        src = kv_ref if e == 0 else window.at[own_slot(e), half]
        return copy(src, window.at[own_slot(e), half], gz_send.at[e], gz_recv.at[e], z_mate)

    def give_sibling(e, own):
        which = half if own else 1 - half
        src = kv_ref if own and e == 0 else window.at[own_slot(e), which]
        slot = 0 if own else 1
        at = last - 1 if e in (0, last) else e - 1
        return copy(
            src, window.at[sibling_slot(e), which], gs_send.at[e, slot], gs_recv.at[at, slot], sibling
        )

    def sibling_wants(e):
        if e == 0:
            return core == 0
        if e == last:
            return jnp.logical_and(has_earlier(e), core == 1)
        return has_earlier(e)

    def send_sibling(e):
        to = last - last * core if e == last else e
        return copy(sib_out.at[e - 1], sib_in.at[to], rs_send.at[e - 1], rs_recv.at[to], sibling)

    def await_sibling_term(e):
        copy(sib_out.at[0], sib_in.at[e], rs_send.at[0], rs_recv.at[e], sibling).wait_recv()

    def send_z(e):
        return copy(z_out.at[e], z_in.at[e], rz_send.at[e], rz_recv.at[e], z_mate)

    def send_far(e):
        return copy(far_out.at[e - 1], far_in.at[e - 1], rd_send.at[e - 1], rd_recv.at[e - 1], earlier(e))

    def send_other(e):
        return copy(z_out.at[e], z_in.at[e], rz_send.at[e], rz_recv.at[e], earlier(e))

    q_in = pltpu.make_async_copy(q_hbm, q_ref, local.at[0])
    up_in = pltpu.make_async_copy(up_hbm, up_ref, local.at[1])
    q_in.start()
    up_in.start()
    barrier = pltpu.get_barrier_semaphore()
    pl.semaphore_signal(barrier, inc=1, device_id=sibling, device_id_type=MESH)
    pl.semaphore_signal(barrier, inc=1, device_id=z_mate, device_id_type=MESH)
    for e in range(1, last + 1):
        @pl.when(has_later(e))
        def _():
            pl.semaphore_signal(barrier, inc=1, device_id=later(e), device_id_type=MESH)

        @pl.when(has_earlier(e))
        def _():
            pl.semaphore_signal(barrier, inc=1, device_id=earlier(e), device_id_type=MESH)

    window[0, half] = kv_ref[...]

    def doc_line(block):
        at = jnp.maximum(block, 0) * lines
        return jnp.concatenate([docs_ref[pl.ds(at + i, 1), :] for i in range(lines)], axis=1)

    sub = lax.broadcasted_iota(jnp.int32, (HEAD, rows), 0)
    row_docs = doc_line(ctx)
    row_weight = jnp.zeros((1, rows), F32)
    for d in range(docs_n):
        row_weight = row_weight + jnp.where(row_docs == d, weight_ref[d], 0.0)
    column_weight = jnp.broadcast_to(row_weight, (HEAD, rows)).T
    ban = jnp.where((sub < docs_n + 1) & (sub != row_docs), -BIG, 0.0).astype(BF16)

    partners = 2 + jnp.minimum(last, chips - 1 - chip) + jnp.minimum(last, chip)
    pl.semaphore_wait(barrier, partners)

    give_z(0).start()
    for e in FAR_EARLY:
        @pl.when(has_later(e))
        def _():
            give_far(e).start()

    @pl.when(core == 0)
    def _():
        give_sibling(0, True).start()

    for slot in range(2 * last + 1):
        if slot == 2 * last:
            block = ctx - 1 - (2 * last - 2) * (1 - core)
        elif slot % 2 == 0 and slot > 0:
            block = ctx - slot + 1 - 2 * core
        else:
            block = ctx - (slot + 1) // 2 * 2
        key_docs = jnp.where(block >= 0, doc_line(block), docs_n)
        keys_x[slot * rows:(slot + 1) * rows, HEAD:] = jnp.where(sub == key_docs, 1.0, 0.0).astype(BF16).T

    q_in.wait()
    up_in.wait()
    for h in range(heads):
        cols = slice(h * HEAD, (h + 1) * HEAD)
        span = slice(h * rows, (h + 1) * rows)
        q_here = q_ref[:, cols]
        q_n[span, :] = q_here
        q_t[:HEAD, span] = q_here.T
        q_t[HEAD:, span] = ban
        weighted = (up_ref[:, cols].astype(F32) * column_weight).astype(BF16)
        up_n[span, :] = weighted
        up_t[:, span] = weighted.T

    for e in FAR_LATE:
        @pl.when(has_later(e))
        def _():
            give_far(e).start()

    def relay_far(e):
        @pl.when(has_earlier(e))
        def _():
            give_far(e).wait_recv()
            if e not in GATHER_BOTH:
                give_z(e).start()

        @pl.when(sibling_wants(e))
        def _():
            give_sibling(e, True).start()

    def relay_other(e):
        if e == 0:
            give_z(0).wait_recv()
            for e_far in GATHER_BOTH:
                @pl.when(has_later(e_far))
                def _():
                    give_other(e_far).start()
        else:
            @pl.when(has_earlier(e))
            def _():
                (give_other(e) if e in GATHER_BOTH else give_z(e)).wait_recv()

        @pl.when(sibling_wants(e))
        def _():
            give_sibling(e, False).start()

    def await_sibling(e):
        for slot in range(2):
            copy(
                kv_ref, window.at[2 * e, 0], gs_send.at[e, slot], gs_recv.at[e - 1, slot], sibling
            ).wait_recv()

    groups = rows // 8

    def exists(e):
        return jnp.logical_or(chip >= e, core == 1) if e == last else chip >= e

    def first_pass(slot):
        first = slot == 0
        span_k = slice(slot * rows, (slot + 1) * rows)
        key = window[slot, 0]
        keys_x[span_k, :HEAD] = key
        keys_t[:, span_k] = key.T
        if first:
            key_at = lax.broadcasted_iota(jnp.int32, (rows, rows), 0)
            row_at = lax.broadcasted_iota(jnp.int32, (rows, rows), 1)
            causal = key_at <= row_at
        for h in range(heads):
            span = slice(h * rows, (h + 1) * rows)
            scores = jnp.dot(keys_x[span_k, :], q_t[:, span], preferred_element_type=F32)
            if first:
                scores = jnp.where(causal, scores, -BIG)
            scores = scores.reshape(groups, 8, rows)
            top = jnp.max(scores, axis=0)
            top = jnp.broadcast_to(jnp.max(top, axis=0, keepdims=True), (8, rows))
            if not first:
                before = top_ref[h]
                top = jnp.maximum(before, top)
                shrink = jnp.exp2((before - top) * LOG2_SCALE)
            top_ref[h] = top
            snap_ref[slot, h] = top
            p = jnp.exp2((scores - top[None]) * LOG2_SCALE)
            dp = jnp.dot(window[slot, 1], up_t[:, span], preferred_element_type=F32).reshape(groups, 8, rows)
            total = jnp.sum(p, axis=0)
            delta = jnp.sum(p * dp, axis=0)
            if not first:
                total = total + total_ref[h] * shrink
                delta = delta + delta_ref[h] * shrink
            total_ref[h] = total
            delta_ref[h] = delta
            p_s[slot, h] = p.reshape(rows, rows)
            dp_s[slot, h] = dp.reshape(rows, rows)

    def first_own(e):
        if e == 0:
            first_pass(0)
            return

        @pl.when(exists(e))
        def _():
            if e == last:
                @pl.when(chip < e)
                def _():
                    window[own_slot(e)] = jnp.zeros((2, rows, HEAD), BF16)

            first_pass(own_slot(e))

    def first_sibling(e):
        @pl.when(exists(e))
        def _():
            await_sibling(e)
            first_pass(2 * e)

    gather_step = {"f": relay_far, "o": relay_other, "a": first_own, "b": first_sibling}
    for step in GATHER_SEQ:
        gather_step[step[0]](int(step[1]))

    for h in range(heads):
        inverse = 1.0 / jnp.broadcast_to(jnp.sum(total_ref[h], axis=0, keepdims=True), (8, rows))
        total_ref[h] = inverse
        delta_ref[h] = inverse * jnp.broadcast_to(
            jnp.sum(delta_ref[h], axis=0, keepdims=True), (8, rows)
        )

    def second_pass(start, count):
        here = slice(start * rows, (start + count) * rows)
        for i in range(count):
            slot = start + i
            for h in range(heads):
                span = slice(h * rows, (h + 1) * rows)
                factor = jnp.exp2((snap_ref[slot, h] - top_ref[h]) * LOG2_SCALE) * total_ref[h]
                probs = p_s[slot, h].reshape(groups, 8, rows) * factor[None]
                grads = probs * (dp_s[slot, h].reshape(groups, 8, rows) - delta_ref[h][None])
                p16[i * rows:(i + 1) * rows, span] = probs.reshape(rows, rows).astype(BF16)
                grad_s[slot * rows:(slot + 1) * rows, span] = grads.reshape(rows, rows).astype(BF16)
        grad_v = jnp.dot(p16[:count * rows], up_n[...], preferred_element_type=F32)
        grad_k = jnp.dot(grad_s[here, :], q_n[...], preferred_element_type=F32) * SCALE
        return grad_k, grad_v

    def second_own(e):
        def body():
            grad_k, grad_v = second_pass(own_slot(e), 1)
            part[e, 0] = grad_k
            part[e, 1] = grad_v

        if e == 0:
            body()
        else:
            pl.when(exists(e))(body)

    def second_missing(e):
        @pl.when(jnp.logical_not(exists(e)))
        def _():
            span_k = slice(own_slot(e) * rows, (own_slot(e) + 2) * rows)
            grad_s[span_k, :] = jnp.zeros((2 * rows, heads * rows), BF16)
            keys_t[:, span_k] = jnp.zeros((HEAD, 2 * rows), BF16)

    def second_sibling(e):
        @pl.when(exists(e))
        def _():
            grad_k, grad_v = second_pass(2 * e, 1)
            sib_out[e - 1, 0] = grad_k
            sib_out[e - 1, 1] = grad_v
            send_sibling(e).start()

        second_missing(e)

    def second_pair(e):
        @pl.when(exists(e))
        def _():
            grad_k, grad_v = second_pass(own_slot(e), 2)
            sib_out[e - 1, 0] = grad_k[rows:]
            sib_out[e - 1, 1] = grad_v[rows:]
            send_sibling(e).start()
            part[e, 0] = grad_k[:rows]
            part[e, 1] = grad_v[:rows]

        second_missing(e)

    def add_sibling_term(e):
        def add():
            await_sibling_term(e)
            part[e] = part[e] + sib_in[e]

        if e == 0:
            pl.when(core == 0)(add)
        elif e == last:
            pl.when(core == 1)(add)
        else:
            add()

    def combine(e):
        if e == 0:
            add_sibling_term(0)
            for e_far in REDUCE_BOTH:
                @pl.when(has_later(e_far))
                def _():
                    send_other(e_far).wait_recv()
                    part[0, 1 - half] = part[0, 1 - half] + z_in[e_far].astype(F32)

            z_out[0] = part[0, 1 - half].astype(BF16)
            send_z(0).start()
            return

        @pl.when(has_earlier(e))
        def _():
            add_sibling_term(e)
            z_out[e] = part[e, 1 - half].astype(BF16)
            if e in REDUCE_BOTH:
                send_other(e).start()
                far_out[e - 1] = part[e, half].astype(BF16)
                send_far(e).start()
            else:
                send_z(e).start()

    def pass_on(e):
        if e in REDUCE_BOTH:
            return

        @pl.when(has_earlier(e))
        def _():
            send_z(e).wait_recv()
            far_out[e - 1] = (part[e, half] + z_in[e].astype(F32)).astype(BF16)
            send_far(e).start()

    def dq_out(h):
        cols = slice(h * HEAD, (h + 1) * HEAD)
        return pltpu.make_async_copy(dq_ref.at[:, cols], dq_hbm.at[:, cols], local.at[2 + h])

    def third_pass(h):
        cols = slice(h * rows, (h + 1) * rows)
        grad = jnp.dot(keys_t[...], grad_s[:, cols], preferred_element_type=F32)
        dq_ref[:, h * HEAD:(h + 1) * HEAD] = (grad.T * SCALE).astype(BF16)
        dq_out(h).start()

    reduce_step = {"a": second_own, "b": second_sibling, "s": second_pair, "c": combine, "g": pass_on, "q": third_pass}
    for step in REDUCE_SEQ:
        reduce_step[step[0]](int(step[1]))
    kept[...] = part[0, half]
    for e in FINAL_ORDER:
        @pl.when(has_later(e))
        def _():
            send_far(e).wait_recv()
            kept[...] = kept[...] + far_in[e - 1].astype(F32)

    send_z(0).wait_recv()
    dkv_ref[...] = (kept[...] + z_in[0].astype(F32)).astype(BF16)

    for h in range(heads):
        dq_out(h).wait()
    give_z(0).wait_send()
    send_z(0).wait_send()
    for e in range(last + 1):
        @pl.when(sibling_wants(e))
        def _():
            give_sibling(e, True).wait_send()
            give_sibling(e, False).wait_send()

        if e > 0:
            @pl.when(has_later(e))
            def _():
                give_far(e).wait_send()
                if e in GATHER_BOTH:
                    give_other(e).wait_send()

            @pl.when(has_earlier(e))
            def _():
                if e not in GATHER_BOTH:
                    give_z(e).wait_send()
                send_far(e).wait_send()
                (send_other(e) if e in REDUCE_BOTH else send_z(e)).wait_send()

            @pl.when(exists(e))
            def _():
                send_sibling(e).wait_send()


def per_device(queries, upstream, key_value, doc_ids, seq_weight):
    rows, width = queries.shape
    heads = width // HEAD
    chips = lax.axis_size("ctx") // 2
    docs_n = seq_weight.shape[0]
    last = CHIPS_BACK
    blocks = 2 * last + 1
    n = heads * rows
    vmem = pltpu.VMEM
    dma = pltpu.SemaphoreType.DMA
    whole = pl.BlockSpec(memory_space=pltpu.VMEM)
    hbm = pl.BlockSpec(memory_space=pl.ANY)
    scratch = [
        vmem(queries.shape, BF16),
        vmem(queries.shape, BF16),
        vmem(queries.shape, BF16),
        vmem((2 * HEAD, n), BF16),
        vmem((HEAD, n), BF16),
        vmem((n, HEAD), BF16),
        vmem((n, HEAD), BF16),
        vmem((blocks, 2, rows, HEAD), BF16),
        vmem((blocks * rows, 2 * HEAD), BF16),
        vmem((HEAD, blocks * rows), BF16),
        vmem((blocks, heads, rows, rows), F32),
        vmem((blocks, heads, rows, rows), F32),
        vmem((2 * rows, n), BF16),
        vmem((blocks * rows, n), BF16),
        vmem((heads, 8, rows), F32),
        vmem((blocks, heads, 8, rows), F32),
        vmem((heads, 8, rows), F32),
        vmem((heads, 8, rows), F32),
        vmem((last + 1, 2, rows, HEAD), F32),
        vmem((last, 2, rows, HEAD), F32),
        vmem((last + 1, 2, rows, HEAD), F32),
        vmem((rows, HEAD), F32),
        vmem((last + 1, rows, HEAD), BF16),
        vmem((last + 1, rows, HEAD), BF16),
        vmem((last, rows, HEAD), BF16),
        vmem((last, rows, HEAD), BF16),
        dma((2 + heads,)),
        dma((last,)), dma((last,)),
        dma((last + 1,)), dma((last + 1,)),
        dma((last + 1, 2)), dma((last, 2)),
        dma((last,)), dma((last + 1,)),
        dma((last + 1,)), dma((last + 1,)),
        dma((last,)), dma((last,)),
    ]
    grads = pl.pallas_call(
        functools.partial(kernel, rows, heads, chips, docs_n),
        out_shape=(
            jax.ShapeDtypeStruct(queries.shape, BF16),
            jax.ShapeDtypeStruct(key_value.shape, BF16),
        ),
        in_specs=[hbm, hbm, whole, whole, pl.BlockSpec(memory_space=pltpu.SMEM)],
        out_specs=(hbm, whole),
        scratch_shapes=scratch,
        compiler_params=pltpu.CompilerParams(
            collective_id=0, has_side_effects=True, vmem_limit_bytes=62 * 2**20
        ),
    )(queries, upstream, key_value, doc_ids.reshape(-1, 128), seq_weight)

    def settle(a, b, x, y):
        x[...] = a[...]
        y[...] = b[...]

    return pl.pallas_call(
        settle,
        out_shape=(
            jax.ShapeDtypeStruct(queries.shape, BF16),
            jax.ShapeDtypeStruct(key_value.shape, BF16),
        ),
        in_specs=[whole, whole],
        out_specs=(whole, whole),
    )(*grads)


def solution(mesh):
    return jax.shard_map(
        per_device,
        mesh=mesh,
        in_specs=(P("ctx", "head"), P("ctx", "head"), P("ctx", "head"), P(), P()),
        out_specs=(P("ctx", "head"), P("ctx", "head")),
        check_vma=False,
    )
```
